512 devices in a mesh: rows: 128 (over y, z, core), heads: 4 (over x).
Axes of the slice: x: 4, y: 8, z: 8, core: 2. Of those that a mesh axis runs over, the one named last changes fastest.
Arguments:
- imagery: bfloat16 [5, 8192, 1024], P(None, 'rows'), may hold values from -120 to 120
- stem_weight: bfloat16 [11520, 1024], P('rows', 'heads'), may hold values from -0.0546875 to 0.0546875
- token_gain: bfloat16 [1024], replicated, may hold values from 0.099609375 to 1.8984375
- latents: bfloat16 [512, 1024], replicated, may hold values from -6 to 6
- latent_gain: bfloat16 [1024], replicated, may hold values from 0.099609375 to 1.8984375
- query_weight: bfloat16 [1024, 1024], P('rows', 'heads'), may hold values from -1.5 to 1.5
- key_weight: bfloat16 [1024, 1024], P('rows', 'heads'), may hold values from -1.5 to 1.5
- value_weight: bfloat16 [1024, 1024], P('rows', 'heads'), may hold values from -0.1875 to 0.1875
- out_weight: bfloat16 [1024, 1024], P('rows', 'heads'), may hold values from -0.1875 to 0.1875
Outputs:
- latent_out: bfloat16 [512, 1024], P('rows', 'heads')
The draws below stay inside these ranges and needn't reach their ends.
All inputs are finite; a program needn't handle non-finite values.
Results may differ from the reference program's by a relative error of at most 0.035.
The reference program's roundings to bfloat16 on the way (of `patches`, `feature`, `token_norm`, `keys`, `values`, `latent_norm`, `queries` and `mixed`) count: a program that leaves them out, or rounds other values in their place, can miss the bound.
Values may be sent and summed in bfloat16 or wider, within the bound.
No kernel may reach another device: no remote copies, remote signals or barrier semaphores. Data moves between devices by JAX's collectives and lax.ppermute only.
A program may use at most 192 MiB of HBM per device.

```python
import math
import jax
import jax.numpy as jnp
from jax import lax

D = 1024
HEADS = 16
LAT = 512
BANDS = 5
KER = 48
STRIDE = 32
KDIM = 11520
TROWS = 2
TCOLS = 32
PIX_ROWS = 8192
PIX_COLS = 1024


def projection_base(key):
    return jnp.clip(jax.random.normal(key, (D, D), jnp.float32), -4.0, 4.0) * (1.7 / math.sqrt(D))


def draw_query_weight(key, part):
    key = jax.random.fold_in(key, 11)
    return projection_base(key).astype(jnp.bfloat16)


def draw_key_weight(key, part):
    key = jax.random.fold_in(key, 12)
    return projection_base(key).astype(jnp.bfloat16)


def draw_imagery(key, part):
    key = jax.random.fold_in(key, 13)
    shape = (BANDS, PIX_ROWS, PIX_COLS)
    row_scale = jnp.exp(jax.random.uniform(jax.random.fold_in(key, 1), (BANDS, PIX_ROWS, 1), jnp.float32, 0.0, math.log(10.0)))
    column_scale = jnp.exp(jax.random.uniform(jax.random.fold_in(key, 2), (BANDS, 1, PIX_COLS), jnp.float32, 0.0, math.log(3.0)))
    noise = jnp.clip(jax.random.normal(jax.random.fold_in(key, 3), shape, jnp.float32), -4.0, 4.0)
    return (noise * row_scale * column_scale).astype(jnp.bfloat16)


def shard_levels(rng, extent, cuts, least, largest):
    def one(axis_at, parts):
        draws = jax.random.uniform(jax.random.fold_in(jax.random.fold_in(rng, 6), axis_at), (parts,), jnp.float32, least / len(cuts), largest / len(cuts))
        return jnp.repeat(jnp.exp(draws), extent[axis_at] // parts).reshape((-1,) + (1,) * (len(extent) - axis_at - 1))

    gain = one(*cuts[0])
    for cut in cuts[1:]:
        gain = gain * one(*cut)
    return gain


def normal_values(stream_key, extent, scale, most, split=(), held_as=jnp.bfloat16):
    drawn = jax.random.normal(stream_key, extent, jnp.float32) * scale
    if len(split) > 0:
        drawn = shard_levels(stream_key, extent, split, -0.22, 0.18) * drawn
    return jnp.clip(drawn, min=-most, max=most).astype(held_as)


def setup_inputs(seed: int = 0) -> dict:
    arg_keys = jax.random.split(jax.random.key(seed), 10)
    imagery = draw_imagery(jax.random.fold_in(arg_keys[9], 71), 0)
    stem_weight = normal_values(arg_keys[1], (KDIM, D), KDIM ** -0.5, 0.0546875, ((0, 128), (1, 4)))
    token_gain = jnp.clip(1.0 + 0.18 * jax.random.normal(arg_keys[2], (D,), jnp.float32), 0.099609375, 1.8984375).astype(jnp.bfloat16)
    latents = normal_values(arg_keys[3], (LAT, D), 1.0, 6.0)
    latent_gain = jnp.clip(1.0 + 0.18 * jax.random.normal(arg_keys[4], (D,), jnp.float32), 0.099609375, 1.8984375).astype(jnp.bfloat16)
    query_weight = draw_query_weight(jax.random.fold_in(arg_keys[9], 71), 0)
    key_weight = draw_key_weight(jax.random.fold_in(arg_keys[9], 71), 0)
    value_weight = normal_values(arg_keys[7], (D, D), D ** -0.5, 0.1875, ((0, 128), (1, 4)))
    out_weight = normal_values(arg_keys[8], (D, D), D ** -0.5, 0.1875, ((0, 128), (1, 4)))
    return {"imagery": imagery, "stem_weight": stem_weight, "token_gain": token_gain, "latents": latents, "latent_gain": latent_gain, "query_weight": query_weight, "key_weight": key_weight, "value_weight": value_weight, "out_weight": out_weight}


epsilon = 1e-05

def layer_norm(inputs, gain_row):
    widened = inputs.astype(jnp.float32)
    average = lax.optimization_barrier(jnp.mean(widened, axis=-1, keepdims=True))
    centered = widened - average
    variance = lax.optimization_barrier(jnp.mean(centered * centered, axis=-1, keepdims=True))
    return (centered * lax.rsqrt(variance + epsilon) * gain_row.astype(jnp.float32)).astype(jnp.bfloat16)

def build_patches(strip_rows):
    rim_rows = KER - STRIDE
    padded = jnp.pad(strip_rows, ((0, 0), (0, STRIDE - rim_rows), (0, STRIDE)))
    blocks = padded.reshape(BANDS, TROWS + 1, STRIDE, TCOLS + 1, STRIDE)
    row_cat = jnp.concatenate([blocks[:, :TROWS], blocks[:, 1:, :rim_rows]], axis=2)
    col_cat = jnp.concatenate([row_cat[:, :, :, :TCOLS, :], row_cat[:, :, :, 1:, :rim_rows]], axis=4)
    ordered = jnp.transpose(col_cat, (1, 3, 0, 2, 4))
    return ordered.reshape(TROWS * TCOLS, BANDS * KER * KER)

def reference(imagery, stem_weight, token_gain, latents, latent_gain, query_weight, key_weight, value_weight, out_weight):
    strip_height = STRIDE * TROWS
    strip_count = imagery.shape[1] // strip_height
    extended = jnp.pad(imagery, ((0, 0), (0, KER - STRIDE), (0, 0)))

    def one_strip(strip_index):
        start_row = (strip_index * strip_height).astype(jnp.int32)
        strip_rows = lax.dynamic_slice_in_dim(extended, start_row, strip_height + KER - STRIDE, 1)
        patches = build_patches(strip_rows)
        feature = jnp.dot(patches, stem_weight, preferred_element_type=jnp.float32).astype(jnp.bfloat16)
        token_norm = layer_norm(feature, token_gain)
        keys = jnp.dot(token_norm, key_weight, preferred_element_type=jnp.float32).astype(jnp.bfloat16)
        values = jnp.dot(token_norm, value_weight, preferred_element_type=jnp.float32).astype(jnp.bfloat16)
        return (keys, values)
    keys, values = lax.map(one_strip, jnp.arange(strip_count, dtype=jnp.int32))
    keys = keys.reshape(-1, D)
    values = values.reshape(-1, D)
    latent_norm = layer_norm(latents, latent_gain)
    queries = jnp.dot(latent_norm, query_weight, preferred_element_type=jnp.float32).astype(jnp.bfloat16)
    head_size = D // HEADS
    score_scale = head_size ** (-0.5)
    query_heads = queries.reshape(LAT, HEADS, head_size).transpose(1, 0, 2)
    key_heads = keys.reshape(-1, HEADS, head_size).transpose(1, 0, 2)
    value_heads = values.reshape(-1, HEADS, head_size).transpose(1, 0, 2)

    def one_head(head_items):
        query_block, key_block, value_block = head_items
        scores = jnp.dot(query_block.astype(jnp.float32), key_block.astype(jnp.float32).T) * score_scale
        maxima = lax.optimization_barrier(jnp.max(scores, axis=1, keepdims=True))
        weights = jnp.exp(scores - maxima)
        totals = lax.optimization_barrier(jnp.sum(weights, axis=1, keepdims=True))
        numerator = jnp.dot(weights, value_block.astype(jnp.float32), precision=lax.Precision.HIGHEST)
        return numerator / totals
    attended = lax.map(one_head, (query_heads, key_heads, value_heads))
    mixed = attended.transpose(1, 0, 2).reshape(LAT, D).astype(jnp.bfloat16)
    return jnp.dot(mixed, out_weight.T, preferred_element_type=jnp.float32).astype(jnp.bfloat16)
```

```python
import jax
import jax.numpy as jnp
from jax import lax
from jax.sharding import Mesh, PartitionSpec as P

D = 1024
HEADS = 16
LAT = 512
BANDS = 5
KER = 48
STRIDE = 32
TROWS = 2
TCOLS = 32
HEAD = D // HEADS

epsilon = 1e-05

ROWS = ("y", "z", "core")
SLOT = 128
STEM_SLOT = 96


def layer_norm(inputs, gain_row):
    widened = inputs.astype(jnp.float32)
    average = jnp.mean(widened, axis=-1, keepdims=True)
    centered = widened - average
    variance = jnp.mean(centered * centered, axis=-1, keepdims=True)
    return (centered * lax.rsqrt(variance + epsilon) * gain_row.astype(jnp.float32)).astype(
        jnp.bfloat16
    )


def build_patches(strip_rows):
    rim_rows = KER - STRIDE
    padded = jnp.pad(strip_rows, ((0, 0), (0, STRIDE - rim_rows), (0, STRIDE)))
    blocks = padded.reshape(BANDS, TROWS + 1, STRIDE, TCOLS + 1, STRIDE)
    row_cat = jnp.concatenate([blocks[:, :TROWS], blocks[:, 1:, :rim_rows]], axis=2)
    col_cat = jnp.concatenate(
        [row_cat[:, :, :, :TCOLS, :], row_cat[:, :, :, 1:, :rim_rows]], axis=4
    )
    ordered = jnp.transpose(col_cat, (1, 3, 0, 2, 4))
    return ordered.reshape(TROWS * TCOLS, BANDS * KER * KER)


def pieces(value):
    high = lax.reduce_precision(value, 8, 7)
    rest = value - high
    middle = lax.reduce_precision(rest, 8, 7)
    return [part.astype(jnp.bfloat16) for part in (high, middle, rest - middle)]


def per_device(
    imagery,
    stem_weight,
    token_gain,
    latents,
    latent_gain,
    query_weight,
    key_weight,
    value_weight,
    out_weight,
):
    rows = lax.axis_size(ROWS)
    rim_rows = KER - STRIDE
    own = stem_weight.shape[0]
    width = stem_weight.shape[1]
    heads_dev = width // HEAD
    latent_dev = LAT // rows

    packed = jnp.concatenate(
        [
            stem_weight,
            jnp.zeros((STEM_SLOT - own, width), jnp.bfloat16),
            query_weight,
            key_weight,
            value_weight,
            out_weight,
        ]
    )
    gathered = lax.all_gather(packed, ROWS, axis=0, tiled=True)

    below = lax.ppermute(imagery[:, :rim_rows, :], ROWS, [(i + 1, i) for i in range(rows - 1)])
    patches = build_patches(jnp.concatenate([imagery, below], axis=1))
    tokens = patches.shape[0]
    patches = jnp.pad(
        patches.reshape(tokens, rows, own), ((0, 0), (0, 0), (0, SLOT - own))
    ).reshape(tokens, rows * SLOT)
    latent_norm = layer_norm(latents, latent_gain)

    feature = jnp.dot(patches, gathered, preferred_element_type=jnp.float32).astype(jnp.bfloat16)
    feature = lax.all_to_all(
        jnp.broadcast_to(feature[None], (4,) + feature.shape), "heads", 0, 0
    )
    feature = jnp.transpose(feature, (1, 0, 2)).reshape(tokens, D)
    token_norm = layer_norm(feature, token_gain)

    slots = gathered.reshape(rows, SLOT, width)

    def projection(index):
        start = STEM_SLOT + 8 * index
        return slots[:, start : start + 8].reshape(D, width)

    queries = jnp.dot(latent_norm, projection(0), preferred_element_type=jnp.float32)
    keys = jnp.dot(token_norm, projection(1), preferred_element_type=jnp.float32)
    values = jnp.dot(token_norm, projection(2), preferred_element_type=jnp.float32)
    query_split = queries.astype(jnp.bfloat16).reshape(LAT, heads_dev, HEAD)
    key_split = keys.astype(jnp.bfloat16).reshape(tokens, heads_dev, HEAD)
    value_split = values.astype(jnp.bfloat16).reshape(tokens, heads_dev, HEAD)
    scores = jnp.einsum(
        "lhd,thd->lht", query_split, key_split, preferred_element_type=jnp.float32
    ) * HEAD ** (-0.5)
    peak = jnp.max(scores, axis=2)
    weights = jnp.exp(scores - peak[:, :, None])
    totals = jnp.sum(weights, axis=2)
    numerator = jnp.einsum(
        "lht,thd->lhd",
        weights.astype(jnp.bfloat16),
        value_split,
        preferred_element_type=jnp.float32,
    ).astype(jnp.bfloat16)

    stats = jnp.stack(pieces(peak) + pieces(totals), axis=1)
    stats = stats.reshape(rows, latent_dev * 6 * heads_dev)
    stats = jnp.pad(stats, ((0, 0), (0, 8 * 128 - stats.shape[1]))).reshape(rows, 8, 128)
    parcel = jnp.concatenate([numerator.reshape(rows, 8, 128), stats], axis=1)
    parcel = lax.all_to_all(parcel, ROWS, 0, 0)

    part = parcel[:, :8].reshape(rows, latent_dev, heads_dev, HEAD).astype(jnp.float32)
    stats = parcel[:, 8:].reshape(rows, 8 * 128)[:, : latent_dev * 6 * heads_dev]
    stats = stats.astype(jnp.float32).reshape(rows, latent_dev, 2, 3, heads_dev)
    stats = stats[:, :, :, 0] + stats[:, :, :, 1] + stats[:, :, :, 2]
    peak, totals = stats[:, :, 0], stats[:, :, 1]
    scale = jnp.exp(peak - jnp.max(peak, axis=0, keepdims=True))
    totals = jnp.sum(scale * totals, axis=0)
    mixed = jnp.sum(scale[..., None] * part, axis=0) / totals[..., None]
    mixed = mixed.reshape(latent_dev, width).astype(jnp.bfloat16)
    out_terms = lax.dot_general(
        mixed, projection(3), (((1,), (1,)), ((), ())), preferred_element_type=jnp.float32
    )
    out_terms = jnp.transpose(out_terms.reshape(latent_dev, 4, width), (1, 0, 2))
    out_terms = lax.all_to_all(out_terms, "heads", 0, 0)
    return jnp.sum(out_terms, axis=0).astype(jnp.bfloat16)


def solution(mesh):
    split = Mesh(mesh.devices.reshape(8, 8, 2, 4), ("y", "z", "core", "heads"))
    spread = P(ROWS, "heads")
    return jax.shard_map(
        per_device,
        mesh=split,
        in_specs=(P(None, ROWS, None), spread, P(), P(), P(), spread, spread, spread, spread),
        out_specs=spread,
        check_vma=False,
    )
```

```python
import jax
import jax.numpy as jnp
from jax import lax
from jax.sharding import Mesh, PartitionSpec as P

D = 1024
HEADS = 16
LAT = 512
BANDS = 5
KER = 48
STRIDE = 32
TROWS = 4
TCOLS = 32
HEAD = D // HEADS

epsilon = 1e-05

ROWS = ("y", "z", "core")
CHIPS = ("y", "z")
SHARE = ("heads", "core")
SLOT = 128
STEM_AT = 32
HALF = 128


def layer_norm(inputs, gain_row):
    widened = inputs.astype(jnp.float32)
    average = jnp.mean(widened, axis=-1, keepdims=True)
    centered = widened - average
    variance = jnp.mean(centered * centered, axis=-1, keepdims=True)
    return (centered * lax.rsqrt(variance + epsilon) * gain_row.astype(jnp.float32)).astype(
        jnp.bfloat16
    )


def build_patches(strip_rows):
    rim_rows = KER - STRIDE
    padded = jnp.pad(strip_rows, ((0, 0), (0, STRIDE - rim_rows), (0, STRIDE)))
    blocks = padded.reshape(BANDS, TROWS + 1, STRIDE, TCOLS + 1, STRIDE)
    row_cat = jnp.concatenate([blocks[:, :TROWS], blocks[:, 1:, :rim_rows]], axis=2)
    col_cat = jnp.concatenate(
        [row_cat[:, :, :, :TCOLS, :], row_cat[:, :, :, 1:, :rim_rows]], axis=4
    )
    ordered = jnp.transpose(col_cat, (1, 3, 0, 2, 4))
    return ordered.reshape(TROWS * TCOLS, BANDS * KER * KER)


def pieces(value):
    high = lax.reduce_precision(value, 8, 7)
    rest = value - high
    middle = lax.reduce_precision(rest, 8, 7)
    return [part.astype(jnp.bfloat16) for part in (high, middle, rest - middle)]


def chip_image(imagery):
    rows = lax.axis_size(ROWS)
    rim = imagery[:, : KER - STRIDE]
    other = lax.ppermute(imagery, "core", [(0, 1), (1, 0)])
    below_even = lax.ppermute(rim, ROWS, [(r + 2, r) for r in range(0, rows - 2, 2)])
    below_odd = lax.ppermute(rim, ROWS, [(r + 1, r) for r in range(1, rows - 2, 2)])
    first = lax.axis_index("core") == 0
    upper = jnp.where(first, imagery, other)
    lower = jnp.where(first, other, imagery)
    below = jnp.where(first, below_even, below_odd)
    return jnp.concatenate([upper, lower, below], axis=1)


def per_device(
    imagery,
    stem_weight,
    token_gain,
    latents,
    latent_gain,
    query_weight,
    key_weight,
    value_weight,
    out_weight,
):
    rows = lax.axis_size(ROWS)
    chips = rows // 2
    own = stem_weight.shape[0]
    width = stem_weight.shape[1]
    heads_core = HALF // HEAD
    latent_chip = LAT // chips

    packed = jnp.concatenate(
        [
            query_weight,
            key_weight,
            value_weight,
            out_weight,
            jnp.pad(stem_weight, ((0, SLOT - STEM_AT - own), (0, 0))),
        ]
    )
    halves = jnp.stack([packed[:, :HALF], packed[:, HALF:]])
    spread = jnp.broadcast_to(halves[None], (8, 2, SLOT, HALF)).reshape(16, SLOT, HALF)
    plane = lax.all_to_all(spread, ("z", "core"), 0, 0)
    gathered = lax.all_gather(plane.reshape(16 * SLOT, HALF), "y", axis=0, tiled=True)

    patches = build_patches(chip_image(imagery))
    tokens = patches.shape[0]
    patches = jnp.pad(
        patches.reshape(tokens, rows, own),
        ((0, 0), (0, 0), (STEM_AT, SLOT - STEM_AT - own)),
    ).reshape(tokens, rows * SLOT)
    latent_norm = layer_norm(latents, latent_gain)

    feature = jnp.dot(patches, gathered, preferred_element_type=jnp.float32).astype(jnp.bfloat16)
    feature = lax.all_to_all(
        jnp.broadcast_to(feature[None], (8,) + feature.shape), SHARE, 0, 0
    )
    feature = jnp.transpose(feature, (1, 0, 2)).reshape(tokens, D)
    token_norm = layer_norm(feature, token_gain)

    slots = gathered.reshape(rows, SLOT, HALF)

    def projection(index):
        return slots[:, 8 * index : 8 * index + 8].reshape(D, HALF)

    queries = jnp.dot(latent_norm, projection(0), preferred_element_type=jnp.float32)
    keys = jnp.dot(token_norm, projection(1), preferred_element_type=jnp.float32)
    values = jnp.dot(token_norm, projection(2), preferred_element_type=jnp.float32)
    query_split = queries.astype(jnp.bfloat16).reshape(LAT, heads_core, HEAD)
    key_split = keys.astype(jnp.bfloat16).reshape(tokens, heads_core, HEAD)
    value_split = values.astype(jnp.bfloat16).reshape(tokens, heads_core, HEAD)
    scores = jnp.einsum(
        "lhd,thd->lht", query_split, key_split, preferred_element_type=jnp.float32
    ) * HEAD ** (-0.5)
    peak = jnp.max(scores, axis=2)
    weights = jnp.exp(scores - peak[:, :, None])
    totals = jnp.sum(weights, axis=2)
    numerator = jnp.einsum(
        "lht,thd->lhd",
        weights.astype(jnp.bfloat16),
        value_split,
        preferred_element_type=jnp.float32,
    ).astype(jnp.bfloat16)

    stats = jnp.stack(pieces(peak) + pieces(totals), axis=2)
    stats = jnp.pad(stats, ((0, 0), (0, 0), (0, HEAD - 6))).reshape(chips, latent_chip, HALF)
    parcel = jnp.concatenate([numerator.reshape(chips, latent_chip, HALF), stats], axis=1)
    parcel = lax.all_to_all(parcel, CHIPS, 0, 0)

    parcel = parcel.astype(jnp.float32).reshape(chips, 2, latent_chip, heads_core, HEAD)
    part, stats = parcel[:, 0], parcel[:, 1]
    peak = stats[..., 0:1] + stats[..., 1:2] + stats[..., 2:3]
    totals = stats[..., 3:4] + stats[..., 4:5] + stats[..., 5:6]
    scale = jnp.exp(peak - jnp.max(peak, axis=0, keepdims=True))
    totals = jnp.sum(scale * totals, axis=0)
    mixed = jnp.sum(scale * part, axis=0) / totals
    mixed = mixed.reshape(latent_chip, HALF).astype(jnp.bfloat16)
    out_terms = lax.dot_general(
        mixed, projection(3), (((1,), (1,)), ((), ())), preferred_element_type=jnp.float32
    )
    out_terms = out_terms.reshape(2, latent_chip // 2, D // width, width)
    out_terms = jnp.transpose(out_terms, (2, 0, 1, 3)).reshape(8, latent_chip // 2, width)
    out_terms = lax.all_to_all(out_terms, SHARE, 0, 0)
    return jnp.sum(out_terms, axis=0).astype(jnp.bfloat16)


def solution(mesh):
    split = Mesh(mesh.devices.reshape(8, 8, 2, 4), ("y", "z", "core", "heads"))
    spread = P(ROWS, "heads")
    return jax.shard_map(
        per_device,
        mesh=split,
        in_specs=(P(None, ROWS, None), spread, P(), P(), P(), spread, spread, spread, spread),
        out_specs=spread,
        check_vma=False,
    )
```
